32 devices in a mesh: req: 2 (over x), head: 4 (over y, core), row: 4 (over z).
Axes of the slice: x: 2, y: 2, z: 4, core: 2. Of those that a mesh axis runs over, the one named last changes fastest.
Arguments:
- incoming_activations: bfloat16 [32, 4, 2048], P(('req', 'head'), None, 'row'), may hold values from -6 to 6
- genuine_symbol_number: int32 [32], replicated, may hold values from 1 to 4, as said below
- caller_sheet_slot: int32 [32], replicated, may hold values from 0 to 31, as said below
- memory_sheets: float32 [32, 32, 4096], P('req', 'head', 'row'), may hold values from -4 to 4
- prior_activation_sheets: float32 [32, 2048], P('req', 'row'), may hold values from -6 to 6
- blend_fractions: float32 [5, 2048], P(None, 'row'), may hold values from 0 to 1
- first_projectors: bfloat16 [3, 2048, 2048], P(None, 'row', 'head'), may hold values from -0.125 to 0.125
- fading_narrow_projector: bfloat16 [2048, 96], P('row'), may hold values from -0.125 to 0.125
- fading_widen_projector: bfloat16 [96, 2048], P(None, 'head'), may hold values from -0.625 to 0.625
- fading_offset: float32 [2048], P('head'), may hold values from -5 to 1
- context_step_narrowing: bfloat16 [2048, 96], P('row'), may hold values from -0.125 to 0.125
- context_step_widening: bfloat16 [96, 2048], P(None, 'head'), may hold values from -0.625 to 0.625
- context_step_offset: float32 [2048], P('head'), may hold values from -2 to 2
- erasure_address_gain: float32 [2048], P('head'), may hold values from 0.25 to 2
- address_correction: float32 [2048], P('head'), may hold values from 0 to 1.5
- reward_coefficients: float32 [32, 64], P('head'), may hold values from -0.6 to 0.6
- groupwise_gain: float32 [32, 64], P('head', 'row'), may hold values from 0.5 to 1.5
- final_projector: bfloat16 [32, 64, 2048], P('head', 'row'), may hold values from -0.125 to 0.125
Outputs:
- mixed: bfloat16 [32, 4, 2048], P(('req', 'head'), None, 'row')
- new_state: float32 [32, 32, 4096], P('req', 'head', 'row')
- new_shift: float32 [32, 2048], P('req', 'row')
The draws below stay inside these ranges and needn't reach their ends.
Inputs may be any that keep to these rules, and one draw needn't show every extreme that they name: `genuine_symbol_number`: every request has 1 or 4 valid tokens; the share with 4 differs between indices of req. `caller_sheet_slot`: a permutation; the pages of index i of req are i * 16 to (i + 1) * 16 - 1; for any two indices of req, between 7 and 8 of the first one's requests have their pages on the second.
All inputs are finite; a program needn't handle non-finite values.
Results may differ from the reference program's by a relative error of at most 0.02.
Values may be sent and summed in bfloat16 or wider, within the bound.
A program may use at most 64 MiB of HBM per device.

```python
import jax
import jax.numpy as jnp
from jax import lax

D = 2048
GROUP_NUMBER = 32
CHANNEL_SPAN = 64
DL = 96
AL = 96
TS = 4
REQ_DEV = 16
REQ = 32


def draw_genuine_symbol_number(key, part):
    groups = REQ // REQ_DEV
    key_share, key_roll, key_fixed = jax.random.split(key, 3)
    long_share = jax.random.randint(key_share, (groups, 1), 0, 9)
    dice_roll = jax.random.randint(key_roll, (groups, REQ_DEV), 0, 8)
    counts = jnp.where(dice_roll < long_share, TS, 1).reshape(-1).astype(jnp.int32)
    chosen = jax.random.randint(key_fixed, (), 0, REQ)
    counts = counts.at[chosen].set(TS)
    counts = counts.at[(chosen + 1) % REQ].set(1)
    return counts


def shuffled(subkey):
    return jax.random.permutation(subkey, REQ_DEV)


def draw_caller_sheet_slot(key, part):
    groups = REQ // REQ_DEV
    key_owner, key_offset, key_rows, key_slots = jax.random.split(key, 4)
    owners = jax.random.permutation(key_owner, groups)
    offsets = jax.random.permutation(key_offset, groups)
    row_perm = jax.vmap(shuffled)(jax.random.split(key_rows, groups))
    slot_perm = jax.vmap(shuffled)(jax.random.split(key_slots, groups))
    device = jnp.arange(groups)[:, None]
    column = jnp.arange(REQ_DEV)[None, :]
    source = owners[(offsets[device] + column) % groups]
    slot_of = slot_perm[source, column]
    pages = (source * REQ_DEV + slot_of).astype(jnp.int32)
    request = device * REQ_DEV + row_perm
    return jnp.zeros((REQ,), jnp.int32).at[request.reshape(-1)].set(pages.reshape(-1))


def level_of(key, extent, pieces, smallest, largest):
    loudness, own = 1.0, jax.random.fold_in(key, 6)
    for axis_at, blocks in pieces:
        heights = jnp.exp(jax.random.uniform(jax.random.fold_in(own, axis_at), (blocks,), jnp.float32, smallest / len(pieces), largest / len(pieces)))
        loudness = loudness * jnp.repeat(heights, extent[axis_at] // blocks).reshape([-1 if axis == axis_at else 1 for axis in range(len(extent))])
    return loudness


def noise(key, shape, spread, bound, cuts=(), held_as=jnp.bfloat16):
    values = jax.random.normal(key, shape, jnp.float32) * spread
    if len(cuts) > 0:
        values = level_of(key, shape, cuts, -0.22, 0.18) * values
    return jnp.clip(values, min=-bound, max=bound).astype(held_as)


def setup_inputs(seed: int = 0) -> dict:
    key_list = jax.random.split(jax.random.key(seed), 19)
    return {
        "incoming_activations": noise(key_list[0], (REQ, TS, D), 1.0, 6.0, ((0, 8), (2, 4))),
        "genuine_symbol_number": draw_genuine_symbol_number(jax.random.fold_in(key_list[18], 71), 0),
        "caller_sheet_slot": draw_caller_sheet_slot(jax.random.fold_in(key_list[18], 71), 0),
        "memory_sheets": noise(key_list[3], (REQ, GROUP_NUMBER, CHANNEL_SPAN * CHANNEL_SPAN), 0.5, 4.0, ((0, 2), (1, 4), (2, 4)), jnp.float32),
        "prior_activation_sheets": noise(key_list[4], (REQ, D), 1.0, 6.0, ((0, 2), (1, 4)), jnp.float32),
        "blend_fractions": jnp.clip(1.0 * jax.random.uniform(key_list[5], (5, D), jnp.float32) ** level_of(key_list[5], (5, D), ((1, 4),), -0.2, 0.2), 0.0, 1.0),
        "first_projectors": noise(key_list[6], (3, D, D), D ** -0.5, 0.125, ((1, 4), (2, 4))),
        "fading_narrow_projector": noise(key_list[7], (D, DL), D ** -0.5, 0.125, ((0, 4),)),
        "fading_widen_projector": noise(key_list[8], (DL, D), DL ** -0.5, 0.625, ((1, 4),)),
        "fading_offset": jnp.clip(-5.0 + 6.0 * jax.random.uniform(key_list[9], (D,), jnp.float32) ** level_of(key_list[9], (D,), ((0, 4),), -0.2, 0.2), -5.0, 1.0),
        "context_step_narrowing": noise(key_list[10], (D, AL), D ** -0.5, 0.125, ((0, 4),)),
        "context_step_widening": noise(key_list[11], (AL, D), AL ** -0.5, 0.625, ((1, 4),)),
        "context_step_offset": jnp.clip(jax.random.uniform(key_list[12], (D,), jnp.float32, -2.0, 2.0) * level_of(key_list[12], (D,), ((0, 4),), -0.4, 0.0), -2.0, 2.0),
        "erasure_address_gain": jnp.clip(0.25 + 1.75 * jax.random.uniform(key_list[13], (D,), jnp.float32) ** level_of(key_list[13], (D,), ((0, 4),), -0.2, 0.2), 0.25, 2.0),
        "address_correction": jnp.clip(1.5 * jax.random.uniform(key_list[14], (D,), jnp.float32) ** level_of(key_list[14], (D,), ((0, 4),), -0.2, 0.2), 0.0, 1.5),
        "reward_coefficients": noise(key_list[15], (GROUP_NUMBER, CHANNEL_SPAN), 0.1, 0.6, ((0, 4),), jnp.float32),
        "groupwise_gain": jnp.clip(0.5 + 1.0 * jax.random.uniform(key_list[16], (GROUP_NUMBER, CHANNEL_SPAN), jnp.float32) ** level_of(key_list[16], (GROUP_NUMBER, CHANNEL_SPAN), ((0, 4), (1, 4)), -0.2, 0.2), 0.5, 1.5),
        "final_projector": noise(key_list[17], (GROUP_NUMBER, CHANNEL_SPAN, D), (GROUP_NUMBER * CHANNEL_SPAN) ** -0.5, 0.125, ((0, 4), (1, 4))),
    }


def project(rows, weight):
    flat = rows.reshape(-1, rows.shape[-1])
    result = jnp.dot(flat, weight, preferred_element_type=jnp.float32)
    return result.reshape(rows.shape[:-1] + (weight.shape[-1],))

def reference(incoming_activations, genuine_symbol_number, caller_sheet_slot, memory_sheets, prior_activation_sheets, blend_fractions, first_projectors, fading_narrow_projector, fading_widen_projector, fading_offset, context_step_narrowing, context_step_widening, context_step_offset, erasure_address_gain, address_correction, reward_coefficients, groupwise_gain, final_projector):
    state_now = memory_sheets[caller_sheet_slot].reshape(REQ, GROUP_NUMBER, CHANNEL_SPAN, CHANNEL_SPAN)
    shift_row = prior_activation_sheets[caller_sheet_slot]
    current = incoming_activations.astype(jnp.float32)
    before = jnp.concatenate([shift_row[:, None, :], current[:, :-1, :]], axis=1)
    towards = before - current
    mixed_in = [(current + towards * blend_fractions[branch]).astype(jnp.bfloat16) for branch in range(5)]
    acceptance_query = project(mixed_in[0], first_projectors[0])
    key_vec = project(mixed_in[2], first_projectors[1])
    payload_entries = project(mixed_in[3], first_projectors[2])
    decay_low = jnp.tanh(project(mixed_in[1], fading_narrow_projector)).astype(jnp.bfloat16)
    log_rate = -jax.nn.softplus(-(fading_offset + project(decay_low, fading_widen_projector))) - 0.5
    decay_rate = jnp.exp(-jnp.exp(log_rate))
    learn_low = project(mixed_in[4], context_step_narrowing).astype(jnp.bfloat16)
    learn_rate = jax.nn.sigmoid(context_step_offset + project(learn_low, context_step_widening))
    heads_shape = (REQ, TS, GROUP_NUMBER, CHANNEL_SPAN)
    scaled = (key_vec * erasure_address_gain).reshape(heads_shape)
    key_dir = scaled / jnp.sqrt(lax.optimization_barrier(jnp.sum(scaled * scaled, axis=-1, keepdims=True)) + 1e-06)
    address_corrected = (key_vec * (1.0 + (learn_rate - 1.0) * address_correction)).reshape(heads_shape)
    acceptance_query = acceptance_query.reshape(heads_shape)
    payload_entries = payload_entries.reshape(heads_shape)
    decay_rate = decay_rate.reshape(heads_shape)
    learn_rate = learn_rate.reshape(heads_shape)
    outputs = []
    for position in range(TS):
        live_now = (position < genuine_symbol_number)[:, None, None, None]
        removed = lax.optimization_barrier(jnp.sum(state_now * (-key_dir[:, position])[:, :, None, :], axis=-1))
        update = state_now * decay_rate[:, position][:, :, None, :]
        update = update + removed[..., None] * (key_dir[:, position] * learn_rate[:, position])[:, :, None, :]
        update = update + payload_entries[:, position][..., None] * address_corrected[:, position][:, :, None, :]
        state_now = jnp.where(live_now, update, state_now)
        reading = lax.optimization_barrier(jnp.sum(state_now * acceptance_query[:, position][:, :, None, :], axis=-1))
        outputs.append(jnp.where(live_now[..., 0], reading, jnp.zeros_like(reading)))
    groupwise_results = jnp.stack(outputs, axis=1)
    genuine_symbol_filter = (jnp.arange(TS)[None, :] < genuine_symbol_number[:, None])[:, :, None, None]
    reward_multiplier = lax.optimization_barrier(jnp.sum(acceptance_query * address_corrected * reward_coefficients, axis=-1, keepdims=True))
    reward_summand = jnp.where(genuine_symbol_filter, reward_multiplier * payload_entries, jnp.zeros_like(payload_entries))
    demeaned_entries = lax.optimization_barrier(jnp.mean(groupwise_results, axis=-1, keepdims=True))
    groupwise_spread = lax.optimization_barrier(jnp.mean((groupwise_results - demeaned_entries) * (groupwise_results - demeaned_entries), axis=-1, keepdims=True))
    standardised_groups = ((groupwise_results - demeaned_entries) / jnp.sqrt(groupwise_spread + 0.00064) * groupwise_gain + reward_summand).astype(jnp.bfloat16)
    mixed = project(standardised_groups.reshape(REQ, TS, GROUP_NUMBER * CHANNEL_SPAN), final_projector.reshape(GROUP_NUMBER * CHANNEL_SPAN, D)).astype(jnp.bfloat16)
    last_token = jnp.take_along_axis(current, (genuine_symbol_number - 1).astype(jnp.int32)[:, None, None], axis=1)[:, 0]
    new_state = jnp.zeros((REQ, GROUP_NUMBER, CHANNEL_SPAN * CHANNEL_SPAN), jnp.float32).at[caller_sheet_slot].set(state_now.reshape(REQ, GROUP_NUMBER, CHANNEL_SPAN * CHANNEL_SPAN))
    new_shift = jnp.zeros((REQ, D), jnp.float32).at[caller_sheet_slot].set(last_token)
    return (mixed, new_state, new_shift)
```

```python
import functools

import jax
import jax.numpy as jnp
from jax import lax
from jax.experimental import pallas as pl
from jax.experimental.pallas import tpu as pltpu
from jax.sharding import PartitionSpec as P

SPAN = 64
TS = 4
F32 = jnp.float32
BF16 = jnp.bfloat16
MESH = pl.DeviceIdType.MESH


def dot(a, b):
    return jnp.dot(a, b, preferred_element_type=F32)


def dot_split(a, ones):
    high = a.astype(BF16)
    low = (a - high.astype(F32)).astype(BF16)
    return dot(high, ones) + dot(low, ones)


def iota2(shape):
    return (
        lax.broadcasted_iota(jnp.int32, shape, 0),
        lax.broadcasted_iota(jnp.int32, shape, 1),
    )


def as_ones(condition):
    return jnp.where(condition, 1.0, 0.0).astype(BF16)


def kernel(
    sizes,
    valid_ref, slot_ref, inv_ref,
    x_ref, pages_hbm, shift_ref, blend_ref, w_hbm, fn_ref, fw_ref, fo_ref,
    cn_ref, cw_ref, co_ref, eg_ref, ac_ref, rc_ref, gg_ref, fp_hbm,
    mixed_ref, state_out, shift_out,
    w_ref, pages_ref, fp_ref,
    x_all, shift_all, pack_out, pack_in, xs_ref, sh_ref, n_ref,
    part_send, part_recv, v_send, v_recv, sum_send, sum_all,
    r_d, kd_d, kl_d, ka_d, dec_d, s_ref, read_ref,
    back_out, back_in, last_all,
    stat_send, stat_recv, out_send, out_recv, fin_send, fin_recv,
    local_sem,
    sx, rx, ssh, rsh, spg, rpg, spt, rpt, sv, rv, ssm, rsm, sst, rst,
    so, ro, sf, rf, sbk, rbk, sla, rla,
):
    R, H, Z = sizes
    RD = pages_ref.shape[0]
    TOK = RD * TS
    BT = TOK // H
    ZT = TOK // Z
    DL = fn_ref.shape[1]
    me_r, me_h, me_z = lax.axis_index("req"), lax.axis_index("head"), lax.axis_index("row")
    pending = []

    def peer(axis, d):
        me, n = {"req": (me_r, R), "head": (me_h, H), "row": (me_z, Z)}[axis]
        return lax.rem(me + d, n)

    def send(src, dst, ssem, rsem, axis, d):
        c = pltpu.make_async_remote_copy(
            src_ref=src, dst_ref=dst, send_sem=ssem.at[d - 1], recv_sem=rsem.at[d - 1],
            device_id={axis: peer(axis, d)}, device_id_type=MESH,
        )
        c.start()
        pending.append(c)
        return c

    loads = [
        pltpu.make_async_copy(pages_hbm, pages_ref, local_sem.at[0]),
        pltpu.make_async_copy(w_hbm, w_ref, local_sem.at[1]),
        pltpu.make_async_copy(fp_hbm, fp_ref, local_sem.at[2]),
    ]
    for c in loads:
        c.start()

    barrier = pltpu.get_barrier_semaphore()
    for axis, n in (("req", R), ("head", H), ("row", Z)):
        for d in range(1, n):
            pl.semaphore_signal(barrier, inc=1, device_id={axis: peer(axis, d)}, device_id_type=MESH)
    pl.semaphore_wait(barrier, R + H + Z - 3)

    xc = [send(x_ref, x_all.at[me_h], sx, rx, "head", d) for d in range(1, H)]
    shc = [send(shift_ref, shift_all.at[pl.ds(me_r * RD, RD)], ssh, rsh, "req", d) for d in range(1, R)]
    x_all[me_h] = x_ref[...]
    shift_all[pl.ds(pl.multiple_of(me_r * RD, RD), RD), :] = shift_ref[...]

    loads[0].wait()
    for p in range(RD):
        page = pages_ref[p]
        half = page.shape[1] // 2
        pack_out[p] = jnp.concatenate([page[:, :half], page[:, half:]], axis=0).astype(BF16)
    pgc = [send(pack_out, pack_in.at[pl.ds(me_r * RD, RD)], spg, rpg, "req", d) for d in range(1, R)]

    row, col = iota2((512, 512))
    same_head = as_ones((row >> 6) == (col >> 6))
    to_rows = as_ones(
        (((row >> 4) & 3) == (col >> 7)) & ((row >> 6) == ((col >> 4) & 7)) & ((row & 15) == (col & 15))
    )
    row, col = iota2((512, 128))
    head_to_feature = as_ones((row >> 6) == (col >> 4))
    row, col = iota2((128, 128))
    half_sum = as_ones((row >> 6) == (col >> 6))
    parity_sum = as_ones((row >> 6) == (col & 1))
    block16 = as_ones((row >> 4) == (col >> 4))
    row, col = iota2((128, 1024))
    spread = as_ones((row & 15) == (col >> 6))
    for r in range(RD):
        n_ref[pl.ds(TS * r, TS), :] = jnp.full((TS, 128), valid_ref[me_r * RD + r], jnp.int32)
    trow, _ = iota2((TOK, 128))
    live = n_ref[...] > (trow & 3)
    live1 = live[:, :1]

    for c in xc + shc:
        c.wait_recv()
    current = x_all[...].reshape(TOK, x_all.shape[2]).astype(F32)
    xs_ref[...] = current
    for r in range(RD):
        sh_ref[pl.ds(TS * r, 1), :] = shift_all[pl.ds(slot_ref[me_r * RD + r], 1), :]
    wide, _ = iota2(current.shape)
    before = jnp.where((wide & 3) == 0, sh_ref[...], pltpu.roll(current, 1, 0))
    towards = before - current
    mixed_in = [(current + towards * blend_ref[b : b + 1, :]).astype(BF16) for b in range(5)]
    d_part = dot(mixed_in[1], fn_ref[...])
    l_part = dot(mixed_in[4], cn_ref[...])
    loads[1].wait()
    r_part = dot(mixed_in[0], w_ref[0])
    k_part = dot(mixed_in[2], w_ref[1])
    fill = jnp.zeros((TOK, 128 - DL), F32)
    part = jnp.concatenate([r_part, k_part, d_part, fill, l_part, fill], axis=1)
    part_send[...] = part.astype(BF16).reshape(part_send.shape)
    ptc = [send(part_send.at[peer("row", d)], part_recv.at[d - 1], spt, rpt, "row", d) for d in range(1, Z)]
    v_part = dot(dot(mixed_in[3], w_ref[2]).astype(BF16), to_rows)
    for q in range(Z):
        v_send[q] = v_part[:, 128 * q : 128 * (q + 1)].astype(BF16)
    vc = [send(v_send.at[peer("row", d)], v_recv.at[d - 1], sv, rv, "row", d) for d in range(1, Z)]

    base = pl.multiple_of(me_r * RD, RD)
    for r in range(RD):
        last_all[pl.ds(base + r, 1), :] = xs_ref[pl.ds(TS * r + jnp.clip(valid_ref[me_r * RD + r] - 1, 0, TS - 1), 1), :]
    lac = [
        send(last_all.at[pl.ds(base, RD)], last_all.at[pl.ds(base, RD)], sla, rla, "req", d)
        for d in range(1, R)
    ]

    total = part_send[me_z].astype(F32)
    for d in range(1, Z):
        ptc[d - 1].wait_recv()
        total = total + part_recv[d - 1].astype(F32)
    sum_send[...] = total.astype(BF16)
    smc = [send(sum_send, sum_all.at[me_z], ssm, rsm, "row", d) for d in range(1, Z)]
    sum_all[me_z] = sum_send[...]

    for c in pgc:
        c.wait_recv()
    for r in range(RD):
        page = slot_ref[me_r * RD + r]
        here = page - me_r * RD
        mine = jnp.logical_and(here >= 0, here < RD)
        own = pages_ref[jnp.clip(here, 0, RD - 1)]
        got = pack_in[page].astype(F32)
        for j in range(8):
            away = got[8 * (j >> 2) : 8 * (j >> 2) + 8, 128 * (j & 3) : 128 * (j & 3) + 128]
            s_ref[j, r] = jnp.where(mine, own[:, 128 * j : 128 * j + 128], away)

    values = v_send[me_z].astype(F32)
    for d in range(1, Z):
        vc[d - 1].wait_recv()
        values = values + v_recv[d - 1].astype(F32)

    for c in smc:
        c.wait_recv()
    sums = sum_all[...].reshape(TOK, sum_all.shape[2]).astype(F32)
    query, key_vec = sums[:, :512], sums[:, 512:1024]
    decay_low = jnp.tanh(sums[:, 1024 : 1024 + DL]).astype(BF16)
    learn_low = sums[:, 1152 : 1152 + DL].astype(BF16)
    z = fo_ref[...] + dot(decay_low, fw_ref[...])
    decay = jnp.exp(-0.6065306597126334 / (1.0 + jnp.exp(-z)))
    y = co_ref[...] + dot(learn_low, cw_ref[...])
    learn = 1.0 / (1.0 + jnp.exp(-y))
    scaled = key_vec * eg_ref[...]
    squares = dot((scaled * scaled).astype(BF16), same_head)
    key_dir = scaled * lax.rsqrt(squares + 1e-6)
    key_adj = key_vec * (1.0 + (learn - 1.0) * ac_ref[...])
    bonus = jnp.where(
        live, dot((query * key_adj * rc_ref[...]).astype(BF16), head_to_feature) * values, 0.0
    )
    lane = lax.broadcasted_iota(jnp.int32, (TOK, 128), 1)
    low_half = lane < 64

    def heads_out(ref, a):
        for p in range(4):
            pair = a[:, 128 * p : 128 * p + 128]
            other = pltpu.roll(pair, 64, 1)
            ref[pl.ds(2 * p, TOK, stride=8), :] = jnp.where(low_half, pair, other)
            ref[pl.ds(2 * p + 1, TOK, stride=8), :] = jnp.where(low_half, other, pair)

    heads_out(r_d, jnp.where(live1, query, 0.0))
    heads_out(kd_d, key_dir)
    heads_out(kl_d, jnp.where(live1, -key_dir * learn, 0.0))
    heads_out(ka_d, jnp.where(live1, key_adj, 0.0))
    heads_out(dec_d, jnp.where(live1, decay, 1.0))

    srow, scol = iota2((8, 128))
    own_head = (scol >> 4) == srow
    values3 = values.reshape(RD, TS, 128)
    for t in range(TS):
        kd, kl, ka, dec, rq = (
            ref[...].reshape(RD, TS, 8, 128)[:, t] for ref in (kd_d, kl_d, ka_d, dec_d, r_d)
        )
        vt = jnp.where(own_head[None], jnp.broadcast_to(values3[:, t][:, None, :], (RD, 8, 128)), 0.0)
        v_wide = dot(vt.reshape(RD * 8, 128).astype(BF16), spread)
        now = [s_ref[j] for j in range(8)]
        hit = dot(
            jnp.concatenate([(s * kd).reshape(RD * 8, 128).astype(BF16) for s in now], axis=0), half_sum
        )
        after = []
        for j in range(8):
            removed = hit[128 * j : 128 * j + 128].reshape(RD, 8, 128)
            vj = v_wide[:, 128 * j : 128 * j + 128].reshape(RD, 8, 128)
            s = now[j] * dec + removed * kl + vj * ka
            s_ref[j] = s
            after.append((s * rq).reshape(RD * 8, 128).astype(BF16))
        seen = dot(jnp.concatenate(after, axis=0), parity_sum)
        acc = jnp.zeros((RD, 8, 128), F32)
        for j in range(8):
            pick = own_head & (((scol & 15) >> 1) == j)
            acc = acc + jnp.where(pick[None], seen[128 * j : 128 * j + 128].reshape(RD, 8, 128), 0.0)
        read_ref[pl.ds(t, RD, stride=TS), :] = jnp.sum(acc, axis=1)

    reading = read_ref[...]
    vrows = 16
    mean_own = dot_split(reading, block16) * (1.0 / vrows)
    off = reading - mean_own
    sq_own = dot_split(off * off, block16)
    is_mean = (lane & 8) == 0
    slot_here = (lane & 7) == (trow & 7)
    packed = jnp.where(slot_here, jnp.where(is_mean, mean_own, sq_own), 0.0)
    stat_send[...] = jnp.sum(packed.reshape(TOK // 8, 8, 128), axis=1)
    stc = [send(stat_send, stat_recv.at[d - 1], sst, rst, "row", d) for d in range(1, Z)]

    for r in range(RD):
        lo = jnp.concatenate([s_ref[j, r] for j in range(4)], axis=1)
        hi = jnp.concatenate([s_ref[j, r] for j in range(4, 8)], axis=1)
        back_out[r] = jnp.concatenate([lo, hi], axis=0).astype(BF16)
    bkc = [send(back_out, back_in.at[pl.ds(me_r * RD, RD)], sbk, rbk, "req", d) for d in range(1, R)]

    packs = [stat_send[...]]
    for d in range(1, Z):
        stc[d - 1].wait_recv()
        packs.append(stat_recv[d - 1])
    both = sum(packs)
    center = both * (1.0 / Z)
    between = sum([(p - center) * (p - center) for p in packs]) * vrows
    spread_all = (both + pltpu.roll(between, 8, 1)) * (1.0 / (vrows * Z))
    _, plane = iota2(both.shape)
    both = jnp.where((plane & 8) == 0, center, lax.rsqrt(spread_all + 64e-5))
    both = jnp.broadcast_to(both[:, None, :], (TOK // 8, 8, 128)).reshape(TOK, 128)
    mean = dot_split(jnp.where(slot_here & is_mean, both, 0.0), block16)
    scale = dot_split(jnp.where(slot_here & jnp.logical_not(is_mean), both, 0.0), block16)
    normed = ((reading - mean) * scale * gg_ref[...] + bonus).astype(BF16)

    loads[2].wait()
    for q in range(Z):
        block = dot(normed, fp_ref[:, 512 * q : 512 * (q + 1)]).astype(BF16)
        for b in range(H):
            out_send[b, q] = block[BT * b : BT * (b + 1)]
    oc = [send(out_send.at[peer("head", d)], out_recv.at[d - 1], so, ro, "head", d) for d in range(1, H)]

    for c in bkc + lac:
        c.wait_recv()
    for p in range(RD):
        q = inv_ref[me_r * RD + p]
        here = q - me_r * RD
        mine = jnp.logical_and(here >= 0, here < RD)
        at = jnp.clip(here, 0, RD - 1)
        got = back_in[q].astype(F32)
        for j in range(8):
            away = got[8 * (j >> 2) : 8 * (j >> 2) + 8, 128 * (j & 3) : 128 * (j & 3) + 128]
            state_out[p, :, 128 * j : 128 * j + 128] = jnp.where(mine, s_ref[j, at], away)
        shift_out[pl.ds(p, 1), :] = last_all[pl.ds(q, 1), :]

    acc = out_send[me_h].astype(F32)
    for d in range(1, H):
        oc[d - 1].wait_recv()
        acc = acc + out_recv[d - 1].astype(F32)
    fin_send[...] = acc.astype(BF16)
    fc = [send(fin_send.at[peer("row", d)], fin_recv.at[d - 1], sf, rf, "row", d) for d in range(1, Z)]
    res = fin_send[me_z].astype(F32)
    for d in range(1, Z):
        fc[d - 1].wait_recv()
        res = res + fin_recv[d - 1].astype(F32)
    mixed_ref[...] = res.astype(BF16)
    for c in pending:
        c.wait_send()


def per_device(x, valid, slots, pages, shift, blend, w, fn, fw, fo, cn, cw, co, eg, ac, rc, gg, fp):
    R, H, Z = lax.axis_size("req"), lax.axis_size("head"), lax.axis_size("row")
    RD, heads, flat = pages.shape
    wide = shift.shape[1]
    TOK = RD * TS
    BT, ZT = TOK // H, TOK // Z
    everyone = jnp.arange(slots.shape[0], dtype=jnp.int32)
    inv = jnp.sum(jnp.where(slots[None, :] == everyone[:, None], everyone[None, :], 0), axis=1)
    feats = gg.shape[0] * gg.shape[1]
    cols = w.shape[2]
    sums = 2 * cols + 256
    smem = pl.BlockSpec(memory_space=pltpu.SMEM)
    vm = pl.BlockSpec(memory_space=pltpu.VMEM)
    hbm = pl.BlockSpec(memory_space=pl.ANY)
    V = pltpu.VMEM
    sems = []
    for n in (H, R, R, Z, Z, Z, Z, H, Z, R, R):
        sems += [pltpu.SemaphoreType.DMA((max(n - 1, 1),))] * 2
    scratch = [
        V(w.shape, BF16), V(pages.shape, F32), V((feats, fp.shape[2]), BF16),
        V((H, BT, wide), BF16), V((R * RD, wide), F32),
        V((RD, 2 * heads, flat // 2), BF16), V((R * RD, 2 * heads, flat // 2), BF16),
        V((TOK, wide), F32), V((TOK, wide), F32), V((TOK, 128), jnp.int32),
        V((Z, ZT, sums), BF16), V((Z - 1, ZT, sums), BF16),
        V((Z, TOK, feats), BF16), V((Z - 1, TOK, feats), BF16),
        V((ZT, sums), BF16), V((Z, ZT, sums), BF16),
        V((TOK * 8, 128), F32), V((TOK * 8, 128), F32), V((TOK * 8, 128), F32),
        V((TOK * 8, 128), F32), V((TOK * 8, 128), F32),
        V((8, RD, 8, 128), F32), V((TOK, 128), F32),
        V((RD, 2 * heads, flat // 2), BF16), V((R * RD, 2 * heads, flat // 2), BF16),
        V((R * RD, wide), F32),
        V((TOK // 8, 128), F32), V((Z - 1, TOK // 8, 128), F32),
        V((H, Z, BT, wide), BF16), V((H - 1, Z, BT, wide), BF16),
        V((Z, BT, wide), BF16), V((Z - 1, BT, wide), BF16),
        pltpu.SemaphoreType.DMA((3,)),
    ] + sems
    mixed, new_state, new_shift = pl.pallas_call(
        functools.partial(kernel, (R, H, Z)),
        out_shape=(
            jax.ShapeDtypeStruct((BT, wide), BF16),
            jax.ShapeDtypeStruct(pages.shape, F32),
            jax.ShapeDtypeStruct(shift.shape, F32),
        ),
        in_specs=[smem] * 3 + [vm, hbm, vm, vm, hbm] + [vm] * 10 + [hbm],
        out_specs=(vm, vm, vm),
        scratch_shapes=scratch,
        compiler_params=pltpu.CompilerParams(
            collective_id=0, has_side_effects=True, vmem_limit_bytes=50 * 1024 * 1024
        ),
    )(
        valid, slots, inv, x.reshape(BT, wide), pages, shift, blend, w, fn, fw,
        fo.reshape(1, -1), cn, cw, co.reshape(1, -1), eg.reshape(1, -1), ac.reshape(1, -1),
        rc.reshape(1, -1), gg.reshape(1, -1), fp.reshape(feats, -1),
    )
    return mixed.reshape(x.shape), new_state, new_shift


def solution(mesh):
    placed = (
        P(("req", "head"), None, "row"),
        P(),
        P(),
        P("req", "head", "row"),
        P("req", "row"),
        P(None, "row"),
        P(None, "row", "head"),
        P("row", None),
        P(None, "head"),
        P("head"),
        P("row", None),
        P(None, "head"),
        P("head"),
        P("head"),
        P("head"),
        P("head", None),
        P("head", "row"),
        P("head", "row", None),
    )
    return jax.shard_map(
        per_device,
        mesh=mesh,
        in_specs=placed,
        out_specs=(P(("req", "head"), None, "row"), P("req", "head", "row"), P("req", "row")),
        check_vma=False,
    )
```

```python
import functools

import jax
import jax.numpy as jnp
from jax import lax
from jax.experimental import pallas as pl
from jax.experimental.pallas import tpu as pltpu
from jax.sharding import PartitionSpec as P

SPAN = 64
TS = 4
F32 = jnp.float32
BF16 = jnp.bfloat16
MESH = pl.DeviceIdType.MESH


def dot(a, b):
    return jnp.dot(a, b, preferred_element_type=F32)


def dot_t(a, b):
    return lax.dot_general(a, b, (((1,), (1,)), ((), ())), preferred_element_type=F32)


def dot_split(a, ones):
    high = a.astype(BF16)
    low = (a - high.astype(F32)).astype(BF16)
    return dot(high, ones) + dot(low, ones)


def iota2(shape):
    return (
        lax.broadcasted_iota(jnp.int32, shape, 0),
        lax.broadcasted_iota(jnp.int32, shape, 1),
    )


def as_ones(condition):
    return jnp.where(condition, 1.0, 0.0).astype(BF16)


def kernel(
    sizes,
    valid_hbm, slot_hbm, x_hbm, pages_hbm, shift_hbm, blend_hbm, w_hbm, fn_hbm, fw_hbm, fo_hbm,
    cn_hbm, cw_hbm, co_hbm, eg_hbm, ac_hbm, rc_hbm, gg_hbm, fp_hbm,
    mixed_ref, state_out, shift_out,
    valid_ref, slot_ref, blend_ref, fn_ref, fw_ref, fo_ref,
    cn_ref, cw_ref, co_ref, eg_ref, ac_ref, rc8_ref, gg8_ref,
    w_ref, pages_ref, fp_ref,
    x_all, shift_all, pack_out, pack_in, xs_ref, sh_ref, n_ref,
    part_send, part_recv, v_send, v_recv, sum_send, sum_all,
    r_d, kd_d, kl_d, ka_d, dec_d, s_ref, read_ref,
    back_out, back_in, last_all,
    stat_send, stat_recv, out_send, out_recv, fin_send, fin_recv,
    local_sem,
    sx, rx, ssh, rsh, spg, rpg, spt, rpt, sv, rv, ssm, rsm, sst, rst,
    so, ro, sf, rf, sbk, rbk, sla, rla,
):
    R, H, Z = sizes
    RD = pages_ref.shape[0]
    TOK = RD * TS
    BT = TOK // H
    ZT = TOK // Z
    DL = fn_ref.shape[0]
    me_r, me_h, me_z = lax.axis_index("req"), lax.axis_index("head"), lax.axis_index("row")
    pending = []

    def peer(axis, d):
        me, n = {"req": (me_r, R), "head": (me_h, H), "row": (me_z, Z)}[axis]
        return lax.rem(me + d, n)

    def send(src, dst, ssem, rsem, axis, d):
        c = pltpu.make_async_remote_copy(
            src_ref=src, dst_ref=dst, send_sem=ssem.at[d - 1], recv_sem=rsem.at[d - 1],
            device_id={axis: peer(axis, d)}, device_id_type=MESH,
        )
        c.start()
        pending.append(c)
        return c

    here_r = pl.multiple_of(me_r * RD, RD)
    loads = [
        pltpu.make_async_copy(src, dst, local_sem.at[i])
        for i, (src, dst) in enumerate([
            (slot_hbm, slot_ref), (valid_hbm, valid_ref), (pages_hbm, pages_ref),
            (x_hbm, x_all.at[me_h]), (shift_hbm, shift_all.at[pl.ds(here_r, RD)]),
            (blend_hbm, blend_ref), (fn_hbm, fn_ref), (cn_hbm, cn_ref), (w_hbm, w_ref),
            (fw_hbm, fw_ref), (cw_hbm, cw_ref), (fo_hbm, fo_ref), (co_hbm, co_ref),
            (eg_hbm, eg_ref), (ac_hbm, ac_ref), (rc_hbm, rc8_ref), (gg_hbm, gg8_ref),
            (fp_hbm, fp_ref),
        ])
    ]
    for c in loads:
        c.start()

    barrier = pltpu.get_barrier_semaphore()
    for axis, n in (("req", R), ("head", H), ("row", Z)):
        for d in range(1, n):
            pl.semaphore_signal(barrier, inc=1, device_id={axis: peer(axis, d)}, device_id_type=MESH)
    pl.semaphore_wait(barrier, R + H + Z - 3)

    xc = [send(x_hbm, x_all.at[me_h], sx, rx, "head", d) for d in range(1, H)]
    shc = [send(shift_hbm, shift_all.at[pl.ds(here_r, RD)], ssh, rsh, "req", d) for d in range(1, R)]
    for c in loads[:3]:
        c.wait()
    for p in range(RD):
        page = pages_ref[p]
        half = page.shape[1] // 2
        pack_out[p] = jnp.concatenate([page[:, :half], page[:, half:]], axis=0).astype(BF16)
    pgc = [send(pack_out, pack_in.at[pl.ds(me_r * RD, RD)], spg, rpg, "req", d) for d in range(1, R)]

    row, col = iota2((512, 512))
    same_head = as_ones((row >> 6) == (col >> 6))
    to_rows = as_ones(
        (((row >> 4) & 3) == (col >> 7)) & ((row >> 6) == ((col >> 4) & 7)) & ((row & 15) == (col & 15))
    )
    row, col = iota2((512, 128))
    head_to_feature = as_ones((row >> 6) == (col >> 4))
    row, col = iota2((128, 128))
    half_sum = as_ones((row >> 6) == (col >> 6))
    parity_sum = as_ones((row >> 6) == (col & 1))
    block16 = as_ones((row >> 4) == (col >> 4))
    row, col = iota2((128, 1024))
    spread = as_ones((row & 15) == (col >> 6))
    for r in range(RD):
        n_ref[pl.ds(TS * r, TS), :] = jnp.full((TS, 128), valid_ref[me_r * RD + r], jnp.int32)
    trow, _ = iota2((TOK, 128))
    live = n_ref[...] > (trow & 3)
    live1 = live[:, :1]

    def find(q, found):
        page = slot_ref[q] - here_r
        return tuple(jnp.where(page == p, q, f) for p, f in enumerate(found))

    inv = lax.fori_loop(0, slot_ref.shape[0], find, (jnp.int32(0),) * RD)

    for c in loads[3:8]:
        c.wait()
    for c in xc + shc:
        c.wait_recv()
    per = x_all.shape[1]
    for r in range(RD):
        xs_ref[pl.ds(TS * r, TS), :] = x_all[r // per, r % per].astype(F32)
    current = xs_ref[...]
    for r in range(RD):
        sh_ref[pl.ds(TS * r, 1), :] = shift_all[pl.ds(slot_ref[me_r * RD + r], 1), :]
    wide, _ = iota2(current.shape)
    before = jnp.where((wide & 3) == 0, sh_ref[...], pltpu.roll(current, 1, 0))
    towards = before - current
    mixed_in = [(current + towards * blend_ref[b : b + 1, :]).astype(BF16) for b in range(5)]
    d_part = dot_t(mixed_in[1], fn_ref[...])
    l_part = dot_t(mixed_in[4], cn_ref[...])
    loads[8].wait()
    r_part = dot(mixed_in[0], w_ref[0])
    k_part = dot(mixed_in[2], w_ref[1])
    fill = jnp.zeros((TOK, 128 - DL), F32)
    part = jnp.concatenate([r_part, k_part, d_part, fill, l_part, fill], axis=1)
    part_send[...] = part.astype(BF16).reshape(part_send.shape)
    ptc = [send(part_send.at[peer("row", d)], part_recv.at[d - 1], spt, rpt, "row", d) for d in range(1, Z)]
    v_part = dot(dot(mixed_in[3], w_ref[2]).astype(BF16), to_rows)
    for q in range(Z):
        v_send[q] = v_part[:, 128 * q : 128 * (q + 1)].astype(BF16)
    vc = [send(v_send.at[peer("row", d)], v_recv.at[d - 1], sv, rv, "row", d) for d in range(1, Z)]

    base = pl.multiple_of(me_r * RD, RD)
    for r in range(RD):
        last_all[pl.ds(base + r, 1), :] = xs_ref[pl.ds(TS * r + jnp.clip(valid_ref[me_r * RD + r] - 1, 0, TS - 1), 1), :]
    lac = [
        send(last_all.at[pl.ds(base, RD)], last_all.at[pl.ds(base, RD)], sla, rla, "req", d)
        for d in range(1, R)
    ]

    total = part_send[me_z].astype(F32)
    for d in range(1, Z):
        ptc[d - 1].wait_recv()
        total = total + part_recv[d - 1].astype(F32)
    sum_send[...] = total.astype(BF16)
    smc = [send(sum_send, sum_all.at[me_z], ssm, rsm, "row", d) for d in range(1, Z)]
    sum_all[me_z] = sum_send[...]

    for c in loads[9:17]:
        c.wait()
    rc_row = jnp.concatenate([rc8_ref[h : h + 1, :] for h in range(8)], axis=1)
    gg_row = jnp.concatenate([gg8_ref[h : h + 1, :] for h in range(8)], axis=1)

    for c in pgc:
        c.wait_recv()
    for r in range(RD):
        page = slot_ref[me_r * RD + r]
        here = page - me_r * RD
        mine = jnp.logical_and(here >= 0, here < RD)
        own = pages_ref[jnp.clip(here, 0, RD - 1)]
        got = pack_in[page].astype(F32)
        for j in range(8):
            away = got[8 * (j >> 2) : 8 * (j >> 2) + 8, 128 * (j & 3) : 128 * (j & 3) + 128]
            s_ref[j, r] = jnp.where(mine, own[:, 128 * j : 128 * j + 128], away)

    values = v_send[me_z].astype(F32)
    for d in range(1, Z):
        vc[d - 1].wait_recv()
        values = values + v_recv[d - 1].astype(F32)

    for c in smc:
        c.wait_recv()
    sums = sum_all[...].reshape(TOK, sum_all.shape[2]).astype(F32)
    query, key_vec = sums[:, :512], sums[:, 512:1024]
    decay_low = jnp.tanh(sums[:, 1024 : 1024 + DL]).astype(BF16)
    learn_low = sums[:, 1152 : 1152 + DL].astype(BF16)
    z = fo_ref[...] + dot(decay_low, fw_ref[...])
    decay = jnp.exp(-0.6065306597126334 / (1.0 + jnp.exp(-z)))
    y = co_ref[...] + dot(learn_low, cw_ref[...])
    learn = 1.0 / (1.0 + jnp.exp(-y))
    scaled = key_vec * eg_ref[...]
    squares = dot((scaled * scaled).astype(BF16), same_head)
    key_dir = scaled * lax.rsqrt(squares + 1e-6)
    key_adj = key_vec * (1.0 + (learn - 1.0) * ac_ref[...])
    bonus = jnp.where(
        live, dot((query * key_adj * rc_row).astype(BF16), head_to_feature) * values, 0.0
    )
    lane = lax.broadcasted_iota(jnp.int32, (TOK, 128), 1)
    low_half = lane < 64

    def heads_out(ref, a):
        for p in range(4):
            pair = a[:, 128 * p : 128 * p + 128]
            other = pltpu.roll(pair, 64, 1)
            ref[pl.ds(2 * p, TOK, stride=8), :] = jnp.where(low_half, pair, other)
            ref[pl.ds(2 * p + 1, TOK, stride=8), :] = jnp.where(low_half, other, pair)

    heads_out(r_d, jnp.where(live1, query, 0.0))
    heads_out(kd_d, key_dir)
    heads_out(kl_d, jnp.where(live1, -key_dir * learn, 0.0))
    heads_out(ka_d, jnp.where(live1, key_adj, 0.0))
    heads_out(dec_d, jnp.where(live1, decay, 1.0))

    srow, scol = iota2((8, 128))
    own_head = (scol >> 4) == srow
    values3 = values.reshape(RD, TS, 128)
    for t in range(TS):
        kd, kl, ka, dec, rq = (
            ref[...].reshape(RD, TS, 8, 128)[:, t] for ref in (kd_d, kl_d, ka_d, dec_d, r_d)
        )
        vt = jnp.where(own_head[None], jnp.broadcast_to(values3[:, t][:, None, :], (RD, 8, 128)), 0.0)
        v_wide = dot(vt.reshape(RD * 8, 128).astype(BF16), spread)
        now = [s_ref[j] for j in range(8)]
        hit = dot(
            jnp.concatenate([(s * kd).reshape(RD * 8, 128).astype(BF16) for s in now], axis=0), half_sum
        )
        after = []
        for j in range(8):
            removed = hit[128 * j : 128 * j + 128].reshape(RD, 8, 128)
            vj = v_wide[:, 128 * j : 128 * j + 128].reshape(RD, 8, 128)
            s = now[j] * dec + removed * kl + vj * ka
            s_ref[j] = s
            after.append((s * rq).reshape(RD * 8, 128).astype(BF16))
        seen = dot(jnp.concatenate(after, axis=0), parity_sum)
        acc = jnp.zeros((RD, 8, 128), F32)
        for j in range(8):
            pick = own_head & (((scol & 15) >> 1) == j)
            acc = acc + jnp.where(pick[None], seen[128 * j : 128 * j + 128].reshape(RD, 8, 128), 0.0)
        read_ref[pl.ds(t, RD, stride=TS), :] = jnp.sum(acc, axis=1)

    reading = read_ref[...]
    vrows = 16
    mean_own = dot_split(reading, block16) * (1.0 / vrows)
    off = reading - mean_own
    sq_own = dot_split(off * off, block16)
    is_mean = (lane & 8) == 0
    slot_here = (lane & 7) == (trow & 7)
    packed = jnp.where(slot_here, jnp.where(is_mean, mean_own, sq_own), 0.0)
    stat_send[...] = jnp.sum(packed.reshape(TOK // 8, 8, 128), axis=1)
    stc = [send(stat_send, stat_recv.at[d - 1], sst, rst, "row", d) for d in range(1, Z)]

    for r in range(RD):
        lo = jnp.concatenate([s_ref[j, r] for j in range(4)], axis=1)
        hi = jnp.concatenate([s_ref[j, r] for j in range(4, 8)], axis=1)
        back_out[r] = jnp.concatenate([lo, hi], axis=0).astype(BF16)
    bkc = [send(back_out, back_in.at[pl.ds(me_r * RD, RD)], sbk, rbk, "req", d) for d in range(1, R)]

    packs = [stat_send[...]]
    for d in range(1, Z):
        stc[d - 1].wait_recv()
        packs.append(stat_recv[d - 1])
    both = sum(packs)
    center = both * (1.0 / Z)
    between = sum([(p - center) * (p - center) for p in packs]) * vrows
    spread_all = (both + pltpu.roll(between, 8, 1)) * (1.0 / (vrows * Z))
    _, plane = iota2(both.shape)
    both = jnp.where((plane & 8) == 0, center, lax.rsqrt(spread_all + 64e-5))
    both = jnp.broadcast_to(both[:, None, :], (TOK // 8, 8, 128)).reshape(TOK, 128)
    mean = dot_split(jnp.where(slot_here & is_mean, both, 0.0), block16)
    scale = dot_split(jnp.where(slot_here & jnp.logical_not(is_mean), both, 0.0), block16)
    normed = ((reading - mean) * scale * gg_row + bonus).astype(BF16)

    loads[17].wait()
    for q in range(Z):
        block = dot(normed, fp_ref[:, 512 * q : 512 * (q + 1)]).astype(BF16)
        for b in range(H):
            out_send[b, q] = block[BT * b : BT * (b + 1)]
    oc = [send(out_send.at[peer("head", d)], out_recv.at[d - 1], so, ro, "head", d) for d in range(1, H)]

    for c in bkc + lac:
        c.wait_recv()
    for p in range(RD):
        q = inv[p]
        here = q - me_r * RD
        mine = jnp.logical_and(here >= 0, here < RD)
        at = jnp.clip(here, 0, RD - 1)
        got = back_in[q].astype(F32)
        for j in range(8):
            away = got[8 * (j >> 2) : 8 * (j >> 2) + 8, 128 * (j & 3) : 128 * (j & 3) + 128]
            state_out[p, :, 128 * j : 128 * j + 128] = jnp.where(mine, s_ref[j, at], away)
        shift_out[pl.ds(p, 1), :] = last_all[pl.ds(q, 1), :]

    acc = out_send[me_h].astype(F32)
    for d in range(1, H):
        oc[d - 1].wait_recv()
        acc = acc + out_recv[d - 1].astype(F32)
    fin_send[...] = acc.astype(BF16)
    fc = [send(fin_send.at[peer("row", d)], fin_recv.at[d - 1], sf, rf, "row", d) for d in range(1, Z)]
    res = fin_send[me_z].astype(F32)
    for d in range(1, Z):
        fc[d - 1].wait_recv()
        res = res + fin_recv[d - 1].astype(F32)
    for i in range(mixed_ref.shape[0]):
        mixed_ref[i] = res[TS * i : TS * (i + 1)].astype(BF16)
    for c in pending:
        c.wait_send()


def per_device(x, valid, slots, pages, shift, blend, w, fn, fw, fo, cn, cw, co, eg, ac, rc, gg, fp):
    R, H, Z = lax.axis_size("req"), lax.axis_size("head"), lax.axis_size("row")
    RD, heads, flat = pages.shape
    wide = shift.shape[1]
    TOK = RD * TS
    BT, ZT = TOK // H, TOK // Z
    feats = gg.shape[0] * gg.shape[1]
    cols = w.shape[2]
    sums = 2 * cols + 256
    vm = pl.BlockSpec(memory_space=pltpu.VMEM)
    hbm = pl.BlockSpec(memory_space=pltpu.HBM)
    V = pltpu.VMEM
    sems = []
    for n in (H, R, R, Z, Z, Z, Z, H, Z, R, R):
        sems += [pltpu.SemaphoreType.DMA((max(n - 1, 1),))] * 2
    fn, cn = fn.T, cn.T
    vec = (1, cols)
    scratch = [
        pltpu.SMEM(valid.shape, jnp.int32), pltpu.SMEM(slots.shape, jnp.int32),
        V(blend.shape, F32), V(fn.shape, BF16), V(fw.shape, BF16), V(vec, F32),
        V(cn.shape, BF16), V(cw.shape, BF16), V(vec, F32), V(vec, F32), V(vec, F32),
        V(rc.shape, F32), V(gg.shape, F32),
        V(w.shape, BF16), V(pages.shape, F32), V((feats, fp.shape[2]), BF16),
        V((H,) + x.shape, BF16), V((R * RD, wide), F32),
        V((RD, 2 * heads, flat // 2), BF16), V((R * RD, 2 * heads, flat // 2), BF16),
        V((TOK, wide), F32), V((TOK, wide), F32), V((TOK, 128), jnp.int32),
        V((Z, ZT, sums), BF16), V((Z - 1, ZT, sums), BF16),
        V((Z, TOK, feats), BF16), V((Z - 1, TOK, feats), BF16),
        V((ZT, sums), BF16), V((Z, ZT, sums), BF16),
        V((TOK * 8, 128), F32), V((TOK * 8, 128), F32), V((TOK * 8, 128), F32),
        V((TOK * 8, 128), F32), V((TOK * 8, 128), F32),
        V((8, RD, 8, 128), F32), V((TOK, 128), F32),
        V((RD, 2 * heads, flat // 2), BF16), V((R * RD, 2 * heads, flat // 2), BF16),
        V((R * RD, wide), F32),
        V((TOK // 8, 128), F32), V((Z - 1, TOK // 8, 128), F32),
        V((H, Z, BT, wide), BF16), V((H - 1, Z, BT, wide), BF16),
        V((Z, BT, wide), BF16), V((Z - 1, BT, wide), BF16),
        pltpu.SemaphoreType.DMA((18,)),
    ] + sems
    mixed, new_state, new_shift = pl.pallas_call(
        functools.partial(kernel, (R, H, Z)),
        out_shape=(
            jax.ShapeDtypeStruct(x.shape, BF16),
            jax.ShapeDtypeStruct(pages.shape, F32),
            jax.ShapeDtypeStruct(shift.shape, F32),
        ),
        in_specs=[hbm] * 18,
        out_specs=(vm, vm, vm),
        scratch_shapes=scratch,
        compiler_params=pltpu.CompilerParams(
            collective_id=0, has_side_effects=True, vmem_limit_bytes=63 * 1024 * 1024
        ),
    )(
        valid, slots, x, pages, shift, blend, w, fn, fw,
        fo.reshape(1, -1), cn, cw, co.reshape(1, -1), eg.reshape(1, -1), ac.reshape(1, -1),
        rc, gg, fp.reshape(feats, -1),
    )
    return mixed, new_state, new_shift


def solution(mesh):
    placed = (
        P(("req", "head"), None, "row"),
        P(),
        P(),
        P("req", "head", "row"),
        P("req", "row"),
        P(None, "row"),
        P(None, "row", "head"),
        P("row", None),
        P(None, "head"),
        P("head"),
        P("row", None),
        P(None, "head"),
        P("head"),
        P("head"),
        P("head"),
        P("head", None),
        P("head", "row"),
        P("head", "row", None),
    )
    return jax.shard_map(
        per_device,
        mesh=mesh,
        in_specs=placed,
        out_specs=(P(("req", "head"), None, "row"), P("req", "head", "row"), P("req", "row")),
        check_vma=False,
    )
```

```python
import functools

import jax
import jax.numpy as jnp
from jax import lax
from jax.experimental import pallas as pl
from jax.experimental.pallas import tpu as pltpu
from jax.sharding import PartitionSpec as P

SPAN = 64
TS = 4
F32 = jnp.float32
BF16 = jnp.bfloat16
MESH = pl.DeviceIdType.MESH


def dot(a, b):
    return jnp.dot(a, b, preferred_element_type=F32)


def dot_t(a, b):
    return lax.dot_general(a, b, (((1,), (1,)), ((), ())), preferred_element_type=F32)


def dot_split(a, ones):
    high = a.astype(BF16)
    low = (a - high.astype(F32)).astype(BF16)
    return dot(high, ones) + dot(low, ones)


def iota2(shape):
    return (
        lax.broadcasted_iota(jnp.int32, shape, 0),
        lax.broadcasted_iota(jnp.int32, shape, 1),
    )


def as_ones(condition):
    return jnp.where(condition, 1.0, 0.0).astype(BF16)


def kernel(
    sizes,
    valid_hbm, slot_hbm, x_hbm, pages_hbm, shift_hbm, blend_hbm, w_hbm, fn_hbm, fw_hbm, fo_hbm,
    cn_hbm, cw_hbm, co_hbm, eg_hbm, ac_hbm, rc_hbm, gg_hbm, fp_hbm,
    mixed_ref, state_out, shift_out,
    valid_ref, slot_ref, blend_ref, fn_ref, fw_ref, fo_ref,
    cn_ref, cw_ref, co_ref, eg_ref, ac_ref, rc8_ref, gg8_ref,
    w_ref, pages_ref, fp_ref, state_buf,
    x_all, shift_all, pack_out, pack_in, xs_ref, sh_ref, n_ref,
    part_send, part_recv, v_send, v_recv, sum_send, sum_all,
    r_d, kd_d, kl_d, ka_d, dec_d, s_ref, read_ref,
    back_out, back_in, last_all,
    stat_send, stat_recv, out_send, out_recv, fin_send, fin_recv,
    local_sem,
    sx, rx, ssh, rsh, spg, rpg, spt, rpt, sv, rv, ssm, rsm, sst, rst,
    so, ro, sf, rf, sbk, rbk, sla, rla,
):
    R, H, Z = sizes
    RD = pages_ref.shape[0]
    TOK = RD * TS
    BT = TOK // H
    ZT = TOK // Z
    DL = fn_ref.shape[0]
    me_r, me_h, me_z = lax.axis_index("req"), lax.axis_index("head"), lax.axis_index("row")
    pending = []

    def peer(axis, d):
        me, n = {"req": (me_r, R), "head": (me_h, H), "row": (me_z, Z)}[axis]
        return lax.rem(me + d, n)

    def send(src, dst, ssem, rsem, axis, d):
        c = pltpu.make_async_remote_copy(
            src_ref=src, dst_ref=dst, send_sem=ssem.at[d - 1], recv_sem=rsem.at[d - 1],
            device_id={axis: peer(axis, d)}, device_id_type=MESH,
        )
        c.start()
        pending.append(c)
        return c

    here_r = pl.multiple_of(me_r * RD, RD)
    loads = [
        pltpu.make_async_copy(src, dst, local_sem.at[i])
        for i, (src, dst) in enumerate([
            (slot_hbm, slot_ref), (valid_hbm, valid_ref), (pages_hbm, pages_ref),
            (x_hbm, x_all.at[me_h]), (shift_hbm, shift_all.at[pl.ds(here_r, RD)]),
            (blend_hbm, blend_ref), (fn_hbm, fn_ref), (cn_hbm, cn_ref), (w_hbm, w_ref),
            (fw_hbm, fw_ref), (cw_hbm, cw_ref), (fo_hbm, fo_ref), (co_hbm, co_ref),
            (eg_hbm, eg_ref), (ac_hbm, ac_ref), (rc_hbm, rc8_ref), (gg_hbm, gg8_ref),
            (fp_hbm, fp_ref),
        ])
    ]
    for c in loads:
        c.start()

    barrier = pltpu.get_barrier_semaphore()
    for axis, n in (("req", R), ("head", H), ("row", Z)):
        for d in range(1, n):
            pl.semaphore_signal(barrier, inc=1, device_id={axis: peer(axis, d)}, device_id_type=MESH)
    pl.semaphore_wait(barrier, R + H + Z - 3)

    xc = [send(x_hbm, x_all.at[me_h], sx, rx, "head", d) for d in range(1, H)]
    shc = [send(shift_hbm, shift_all.at[pl.ds(here_r, RD)], ssh, rsh, "req", d) for d in range(1, R)]
    for c in loads[:3]:
        c.wait()
    for p in range(RD):
        page = pages_ref[p]
        half = page.shape[1] // 2
        pack_out[p] = jnp.concatenate([page[:, :half], page[:, half:]], axis=0).astype(BF16)
    pgc = [send(pack_out, pack_in.at[pl.ds(me_r * RD, RD)], spg, rpg, "req", d) for d in range(1, R)]

    for r in range(RD):
        n_ref[pl.ds(TS * r, TS), :] = jnp.full((TS, 128), valid_ref[me_r * RD + r], jnp.int32)
    trow, _ = iota2((TOK, 128))
    live = n_ref[...] > (trow & 3)
    live1 = live[:, :1]

    for c in loads[3:8]:
        c.wait()
    for c in xc + shc:
        c.wait_recv()
    per = x_all.shape[1]
    for r in range(RD):
        xs_ref[pl.ds(TS * r, TS), :] = x_all[r // per, r % per].astype(F32)
    current = xs_ref[...]
    for r in range(RD):
        sh_ref[pl.ds(TS * r, 1), :] = shift_all[pl.ds(slot_ref[me_r * RD + r], 1), :]
    wide, _ = iota2(current.shape)
    before = jnp.where((wide & 3) == 0, sh_ref[...], pltpu.roll(current, 1, 0))
    towards = before - current
    mixed_in = [(current + towards * blend_ref[b : b + 1, :]).astype(BF16) for b in range(5)]
    d_part = dot_t(mixed_in[1], fn_ref[...])
    l_part = dot_t(mixed_in[4], cn_ref[...])
    loads[8].wait()
    r_part = dot(mixed_in[0], w_ref[0])
    k_part = dot(mixed_in[2], w_ref[1])
    fill = jnp.zeros((TOK, 128 - DL), F32)
    part = jnp.concatenate([r_part, k_part, d_part, fill, l_part, fill], axis=1)
    part_send[...] = part.astype(BF16).reshape(part_send.shape)
    ptc = [send(part_send.at[peer("row", d)], part_recv.at[d - 1], spt, rpt, "row", d) for d in range(1, Z)]
    row, col = iota2((512, 512))
    to_rows = as_ones(
        (((row >> 4) & 3) == (col >> 7)) & ((row >> 6) == ((col >> 4) & 7)) & ((row & 15) == (col & 15))
    )
    v_part = dot(dot(mixed_in[3], w_ref[2]).astype(BF16), to_rows)
    for q in range(Z):
        v_send[q] = v_part[:, 128 * q : 128 * (q + 1)].astype(BF16)
    vc = [send(v_send.at[peer("row", d)], v_recv.at[d - 1], sv, rv, "row", d) for d in range(1, Z)]

    base = pl.multiple_of(me_r * RD, RD)
    for r in range(RD):
        last_all[pl.ds(base + r, 1), :] = xs_ref[pl.ds(TS * r + jnp.clip(valid_ref[me_r * RD + r] - 1, 0, TS - 1), 1), :]
    lac = [
        send(last_all.at[pl.ds(base, RD)], last_all.at[pl.ds(base, RD)], sla, rla, "req", d)
        for d in range(1, R)
    ]

    row, col = iota2((512, 512))
    same_head = as_ones((row >> 6) == (col >> 6))
    row, col = iota2((512, 128))
    head_to_feature = as_ones((row >> 6) == (col >> 4))
    row, col = iota2((128, 128))
    half_sum = as_ones((row >> 6) == (col >> 6))
    parity_sum = as_ones((row >> 6) == (col & 1))
    block16 = as_ones((row >> 4) == (col >> 4))
    row, col = iota2((128, 1024))
    spread = as_ones((row & 15) == (col >> 6))
    def find(q, found):
        page = slot_ref[q] - here_r
        return tuple(jnp.where(page == p, q, f) for p, f in enumerate(found))

    inv = lax.fori_loop(0, slot_ref.shape[0], find, (jnp.int32(0),) * RD)

    total = part_send[me_z].astype(F32)
    for d in range(1, Z):
        ptc[d - 1].wait_recv()
        total = total + part_recv[d - 1].astype(F32)
    sum_send[...] = total.astype(BF16)
    smc = [send(sum_send, sum_all.at[me_z], ssm, rsm, "row", d) for d in range(1, Z)]
    sum_all[me_z] = sum_send[...]

    for c in loads[9:17]:
        c.wait()
    rc_row = jnp.concatenate([rc8_ref[h : h + 1, :] for h in range(8)], axis=1)
    gg_row = jnp.concatenate([gg8_ref[h : h + 1, :] for h in range(8)], axis=1)

    for c in pgc:
        c.wait_recv()
    for r in range(RD):
        page = slot_ref[me_r * RD + r]
        here = page - me_r * RD
        mine = jnp.logical_and(here >= 0, here < RD)
        own = pages_ref[jnp.clip(here, 0, RD - 1)]
        got = pack_in[page].astype(F32)
        for j in range(8):
            away = got[8 * (j >> 2) : 8 * (j >> 2) + 8, 128 * (j & 3) : 128 * (j & 3) + 128]
            s_ref[j, r] = jnp.where(mine, own[:, 128 * j : 128 * j + 128], away)

    values = v_send[me_z].astype(F32)
    for d in range(1, Z):
        vc[d - 1].wait_recv()
        values = values + v_recv[d - 1].astype(F32)

    for c in smc:
        c.wait_recv()
    sums = sum_all[...].reshape(TOK, sum_all.shape[2]).astype(F32)
    query, key_vec = sums[:, :512], sums[:, 512:1024]
    decay_low = jnp.tanh(sums[:, 1024 : 1024 + DL]).astype(BF16)
    learn_low = sums[:, 1152 : 1152 + DL].astype(BF16)
    z = fo_ref[...] + dot(decay_low, fw_ref[...])
    decay = jnp.exp(-0.6065306597126334 / (1.0 + jnp.exp(-z)))
    y = co_ref[...] + dot(learn_low, cw_ref[...])
    learn = 1.0 / (1.0 + jnp.exp(-y))
    scaled = key_vec * eg_ref[...]
    squares = dot((scaled * scaled).astype(BF16), same_head)
    key_dir = scaled * lax.rsqrt(squares + 1e-6)
    key_adj = key_vec * (1.0 + (learn - 1.0) * ac_ref[...])
    bonus = jnp.where(
        live, dot((query * key_adj * rc_row).astype(BF16), head_to_feature) * values, 0.0
    )
    lane = lax.broadcasted_iota(jnp.int32, (TOK, 128), 1)
    low_half = lane < 64

    def heads_out(ref, a):
        for p in range(4):
            pair = a[:, 128 * p : 128 * p + 128]
            other = pltpu.roll(pair, 64, 1)
            ref[pl.ds(2 * p, TOK, stride=8), :] = jnp.where(low_half, pair, other)
            ref[pl.ds(2 * p + 1, TOK, stride=8), :] = jnp.where(low_half, other, pair)

    heads_out(r_d, jnp.where(live1, query, 0.0))
    heads_out(kd_d, key_dir)
    heads_out(kl_d, jnp.where(live1, -key_dir * learn, 0.0))
    heads_out(ka_d, jnp.where(live1, key_adj, 0.0))
    heads_out(dec_d, jnp.where(live1, decay, 1.0))

    srow, scol = iota2((8, 128))
    own_head = (scol >> 4) == srow
    values3 = values.reshape(RD, TS, 128)
    for t in range(TS):
        kd, kl, ka, dec, rq = (
            ref[...].reshape(RD, TS, 8, 128)[:, t] for ref in (kd_d, kl_d, ka_d, dec_d, r_d)
        )
        vt = jnp.where(own_head[None], jnp.broadcast_to(values3[:, t][:, None, :], (RD, 8, 128)), 0.0)
        v_wide = dot(vt.reshape(RD * 8, 128).astype(BF16), spread)
        now = [s_ref[j] for j in range(8)]
        hit = dot(
            jnp.concatenate([(s * kd).reshape(RD * 8, 128).astype(BF16) for s in now], axis=0), half_sum
        )
        after = []
        for j in range(8):
            removed = hit[128 * j : 128 * j + 128].reshape(RD, 8, 128)
            vj = v_wide[:, 128 * j : 128 * j + 128].reshape(RD, 8, 128)
            s = now[j] * dec + removed * kl + vj * ka
            s_ref[j] = s
            after.append((s * rq).reshape(RD * 8, 128).astype(BF16))
        seen = dot(jnp.concatenate(after, axis=0), parity_sum)
        acc = jnp.zeros((RD, 8, 128), F32)
        for j in range(8):
            pick = own_head & (((scol & 15) >> 1) == j)
            acc = acc + jnp.where(pick[None], seen[128 * j : 128 * j + 128].reshape(RD, 8, 128), 0.0)
        read_ref[pl.ds(t, RD, stride=TS), :] = jnp.sum(acc, axis=1)

    reading = read_ref[...]
    vrows = 16
    mean_own = dot_split(reading, block16) * (1.0 / vrows)
    off = reading - mean_own
    sq_own = dot_split(off * off, block16)
    is_mean = (lane & 8) == 0
    slot_here = (lane & 7) == (trow & 7)
    packed = jnp.where(slot_here, jnp.where(is_mean, mean_own, sq_own), 0.0)
    stat_send[...] = jnp.sum(packed.reshape(TOK // 8, 8, 128), axis=1)
    stc = [send(stat_send, stat_recv.at[d - 1], sst, rst, "row", d) for d in range(1, Z)]

    for r in range(RD):
        lo = jnp.concatenate([s_ref[j, r] for j in range(4)], axis=1)
        hi = jnp.concatenate([s_ref[j, r] for j in range(4, 8)], axis=1)
        back_out[r] = jnp.concatenate([lo, hi], axis=0).astype(BF16)
    bkc = [send(back_out, back_in.at[pl.ds(me_r * RD, RD)], sbk, rbk, "req", d) for d in range(1, R)]

    packs = [stat_send[...]]
    for d in range(1, Z):
        stc[d - 1].wait_recv()
        packs.append(stat_recv[d - 1])
    both = sum(packs)
    center = both * (1.0 / Z)
    between = sum([(p - center) * (p - center) for p in packs]) * vrows
    spread_all = (both + pltpu.roll(between, 8, 1)) * (1.0 / (vrows * Z))
    _, plane = iota2(both.shape)
    both = jnp.where((plane & 8) == 0, center, lax.rsqrt(spread_all + 64e-5))
    both = jnp.broadcast_to(both[:, None, :], (TOK // 8, 8, 128)).reshape(TOK, 128)
    mean = dot_split(jnp.where(slot_here & is_mean, both, 0.0), block16)
    scale = dot_split(jnp.where(slot_here & jnp.logical_not(is_mean), both, 0.0), block16)
    normed = ((reading - mean) * scale * gg_row + bonus).astype(BF16)

    loads[17].wait()
    for q in range(Z):
        block = dot(normed, fp_ref[:, 512 * q : 512 * (q + 1)]).astype(BF16)
        for b in range(H):
            out_send[b, q] = block[BT * b : BT * (b + 1)]
    oc = [send(out_send.at[peer("head", d)], out_recv.at[d - 1], so, ro, "head", d) for d in range(1, H)]

    acc = out_send[me_h].astype(F32)
    for d in range(1, H):
        oc[d - 1].wait_recv()
        acc = acc + out_recv[d - 1].astype(F32)
    fin_send[...] = acc.astype(BF16)
    fc = [send(fin_send.at[peer("row", d)], fin_recv.at[d - 1], sf, rf, "row", d) for d in range(1, Z)]
    for c in bkc + lac:
        c.wait_recv()
    for p in range(RD):
        q = inv[p]
        here = q - me_r * RD
        mine = jnp.logical_and(here >= 0, here < RD)
        at = jnp.clip(here, 0, RD - 1)
        got = back_in[q].astype(F32)
        for j in range(8):
            away = got[8 * (j >> 2) : 8 * (j >> 2) + 8, 128 * (j & 3) : 128 * (j & 3) + 128]
            state_buf[p, :, 128 * j : 128 * j + 128] = jnp.where(mine, s_ref[j, at], away)
        shift_out[pl.ds(p, 1), :] = last_all[pl.ds(q, 1), :]

    stored = pltpu.make_async_copy(state_buf, state_out, local_sem.at[18])
    stored.start()

    res = fin_send[me_z].astype(F32)
    for d in range(1, Z):
        fc[d - 1].wait_recv()
        res = res + fin_recv[d - 1].astype(F32)
    for i in range(mixed_ref.shape[0]):
        mixed_ref[i] = res[TS * i : TS * (i + 1)].astype(BF16)
    stored.wait()
    for c in pending:
        c.wait_send()


def hand_on(a, b, c, a_out, b_out, c_out, sem):
    copies = [
        pltpu.make_async_copy(src, dst, sem.at[i])
        for i, (src, dst) in enumerate([(b, b_out), (a, a_out), (c, c_out)])
    ]
    for copy in copies:
        copy.start()
    for copy in copies:
        copy.wait()


def per_device(x, valid, slots, pages, shift, blend, w, fn, fw, fo, cn, cw, co, eg, ac, rc, gg, fp):
    R, H, Z = lax.axis_size("req"), lax.axis_size("head"), lax.axis_size("row")
    RD, heads, flat = pages.shape
    wide = shift.shape[1]
    TOK = RD * TS
    BT, ZT = TOK // H, TOK // Z
    feats = gg.shape[0] * gg.shape[1]
    cols = w.shape[2]
    sums = 2 * cols + 256
    vm = pl.BlockSpec(memory_space=pltpu.VMEM)
    hbm = pl.BlockSpec(memory_space=pltpu.HBM)
    V = pltpu.VMEM
    sems = []
    for n in (H, R, R, Z, Z, Z, Z, H, Z, R, R):
        sems += [pltpu.SemaphoreType.DMA((max(n - 1, 1),))] * 2
    fn, cn = fn.T, cn.T
    vec = (1, cols)
    scratch = [
        pltpu.SMEM(valid.shape, jnp.int32), pltpu.SMEM(slots.shape, jnp.int32),
        V(blend.shape, F32), V(fn.shape, BF16), V(fw.shape, BF16), V(vec, F32),
        V(cn.shape, BF16), V(cw.shape, BF16), V(vec, F32), V(vec, F32), V(vec, F32),
        V(rc.shape, F32), V(gg.shape, F32),
        V(w.shape, BF16), V(pages.shape, F32), V((feats, fp.shape[2]), BF16),
        V(pages.shape, F32),
        V((H,) + x.shape, BF16), V((R * RD, wide), F32),
        V((RD, 2 * heads, flat // 2), BF16), V((R * RD, 2 * heads, flat // 2), BF16),
        V((TOK, wide), F32), V((TOK, wide), F32), V((TOK, 128), jnp.int32),
        V((Z, ZT, sums), BF16), V((Z - 1, ZT, sums), BF16),
        V((Z, TOK, feats), BF16), V((Z - 1, TOK, feats), BF16),
        V((ZT, sums), BF16), V((Z, ZT, sums), BF16),
        V((TOK * 8, 128), F32), V((TOK * 8, 128), F32), V((TOK * 8, 128), F32),
        V((TOK * 8, 128), F32), V((TOK * 8, 128), F32),
        V((8, RD, 8, 128), F32), V((TOK, 128), F32),
        V((RD, 2 * heads, flat // 2), BF16), V((R * RD, 2 * heads, flat // 2), BF16),
        V((R * RD, wide), F32),
        V((TOK // 8, 128), F32), V((Z - 1, TOK // 8, 128), F32),
        V((H, Z, BT, wide), BF16), V((H - 1, Z, BT, wide), BF16),
        V((Z, BT, wide), BF16), V((Z - 1, BT, wide), BF16),
        pltpu.SemaphoreType.DMA((19,)),
    ] + sems
    results = pl.pallas_call(
        functools.partial(kernel, (R, H, Z)),
        out_shape=(
            jax.ShapeDtypeStruct(x.shape, BF16),
            jax.ShapeDtypeStruct(pages.shape, F32),
            jax.ShapeDtypeStruct(shift.shape, F32),
        ),
        in_specs=[hbm] * 18,
        out_specs=(vm, hbm, vm),
        scratch_shapes=scratch,
        compiler_params=pltpu.CompilerParams(
            collective_id=0, has_side_effects=True, vmem_limit_bytes=63 * 1024 * 1024
        ),
    )(
        valid, slots, x, pages, shift, blend, w, fn, fw,
        fo.reshape(1, -1), cn, cw, co.reshape(1, -1), eg.reshape(1, -1), ac.reshape(1, -1),
        rc, gg, fp.reshape(feats, -1),
    )
    return pl.pallas_call(
        hand_on,
        out_shape=tuple(jax.ShapeDtypeStruct(a.shape, a.dtype) for a in results),
        in_specs=[hbm] * 3,
        out_specs=(hbm,) * 3,
        scratch_shapes=[pltpu.SemaphoreType.DMA((3,))],
        compiler_params=pltpu.CompilerParams(vmem_limit_bytes=63 * 1024 * 1024),
    )(*results)


def solution(mesh):
    placed = (
        P(("req", "head"), None, "row"),
        P(),
        P(),
        P("req", "head", "row"),
        P("req", "row"),
        P(None, "row"),
        P(None, "row", "head"),
        P("row", None),
        P(None, "head"),
        P("head"),
        P("row", None),
        P(None, "head"),
        P("head"),
        P("head"),
        P("head"),
        P("head", None),
        P("head", "row"),
        P("head", "row", None),
    )
    return jax.shard_map(
        per_device,
        mesh=mesh,
        in_specs=placed,
        out_specs=(P(("req", "head"), None, "row"), P("req", "head", "row"), P("req", "row")),
        check_vma=False,
    )
```

```python
import functools

import jax
import jax.numpy as jnp
from jax import lax
from jax.experimental import pallas as pl
from jax.experimental.pallas import tpu as pltpu
from jax.sharding import PartitionSpec as P

SPAN = 64
TS = 4
F32 = jnp.float32
BF16 = jnp.bfloat16
MESH = pl.DeviceIdType.MESH


def dot(a, b):
    return jnp.dot(a, b, preferred_element_type=F32)


def dot_t(a, b):
    return lax.dot_general(a, b, (((1,), (1,)), ((), ())), preferred_element_type=F32)


def dot_split(a, ones):
    high = a.astype(BF16)
    low = (a - high.astype(F32)).astype(BF16)
    return dot(high, ones) + dot(low, ones)


def iota2(shape):
    return (
        lax.broadcasted_iota(jnp.int32, shape, 0),
        lax.broadcasted_iota(jnp.int32, shape, 1),
    )


def as_ones(condition):
    return jnp.where(condition, 1.0, 0.0).astype(BF16)


def kernel(
    sizes,
    valid_hbm, slot_hbm, x_hbm, pages_hbm, shift_hbm, blend_hbm, w_hbm, fn_hbm, fw_hbm, fo_hbm,
    cn_hbm, cw_hbm, co_hbm, eg_hbm, ac_hbm, rc_hbm, gg_hbm, fp_hbm,
    mixed_ref, state_out, shift_out,
    valid_ref, slot_ref, blend_ref, fn_ref, fw_ref, fo_ref,
    cn_ref, cw_ref, co_ref, eg_ref, ac_ref, rc8_ref, gg8_ref,
    w_ref, pages_ref, fp_ref, state_buf,
    x_all, shift_all, pack_out, pack_in, xs_ref, sh_ref, n_ref,
    part_send, part_recv, v_send, v_recv, sum_send, sum_all,
    r_d, kd_d, kl_d, ka_d, dec_d, s_ref, read_ref,
    back_out, back_in, last_all,
    stat_send, stat_recv, out_send, out_recv, fin_send, fin_recv,
    local_sem,
    sx, rx, ssh, rsh, spg, rpg, spt, rpt, sv, rv, ssm, rsm, sst, rst,
    so, ro, sf, rf, sbk, rbk, sla, rla,
):
    R, H, Z = sizes
    RD = pages_ref.shape[0]
    TOK = RD * TS
    BT = TOK // H
    ZT = TOK // Z
    DL = fn_ref.shape[0]
    me_r, me_h, me_z = lax.axis_index("req"), lax.axis_index("head"), lax.axis_index("row")
    pending = []

    def peer(axis, d):
        me, n = {"req": (me_r, R), "head": (me_h, H), "row": (me_z, Z)}[axis]
        return lax.rem(me + d, n)

    def send(src, dst, ssem, rsem, axis, d):
        c = pltpu.make_async_remote_copy(
            src_ref=src, dst_ref=dst, send_sem=ssem.at[d - 1], recv_sem=rsem.at[d - 1],
            device_id={axis: peer(axis, d)}, device_id_type=MESH,
        )
        c.start()
        pending.append(c)
        return c

    here_r = pl.multiple_of(me_r * RD, RD)
    loads = [
        pltpu.make_async_copy(src, dst, local_sem.at[i])
        for i, (src, dst) in enumerate([
            (slot_hbm, slot_ref), (valid_hbm, valid_ref), (pages_hbm, pages_ref),
            (x_hbm, x_all.at[me_h]), (shift_hbm, shift_all.at[pl.ds(here_r, RD)]),
            (blend_hbm, blend_ref), (fn_hbm, fn_ref), (cn_hbm, cn_ref), (w_hbm, w_ref),
            (fw_hbm, fw_ref), (cw_hbm, cw_ref), (fo_hbm, fo_ref), (co_hbm, co_ref),
            (eg_hbm, eg_ref), (ac_hbm, ac_ref), (rc_hbm, rc8_ref), (gg_hbm, gg8_ref),
            (fp_hbm, fp_ref),
        ])
    ]
    for c in loads:
        c.start()

    barrier = pltpu.get_barrier_semaphore()
    for axis, n in (("req", R), ("head", H), ("row", Z)):
        for d in range(1, n):
            pl.semaphore_signal(barrier, inc=1, device_id={axis: peer(axis, d)}, device_id_type=MESH)
    pl.semaphore_wait(barrier, R + H + Z - 3)

    xc = [send(x_hbm, x_all.at[me_h], sx, rx, "head", d) for d in range(1, H)]
    shc = [send(shift_hbm, shift_all.at[pl.ds(here_r, RD)], ssh, rsh, "req", d) for d in range(1, R)]
    for c in loads[:3]:
        c.wait()
    for p in range(RD):
        page = pages_ref[p]
        half = page.shape[1] // 2
        pack_out[p] = jnp.concatenate([page[:, :half], page[:, half:]], axis=0).astype(BF16)
    pgc = [send(pack_out, pack_in.at[pl.ds(me_r * RD, RD)], spg, rpg, "req", d) for d in range(1, R)]

    for r in range(RD):
        n_ref[pl.ds(TS * r, TS), :] = jnp.full((TS, 128), valid_ref[me_r * RD + r], jnp.int32)
    trow, _ = iota2((TOK, 128))
    live = n_ref[...] > (trow & 3)
    live1 = live[:, :1]

    for c in loads[3:8]:
        c.wait()
    for c in xc + shc:
        c.wait_recv()
    per = x_all.shape[1]
    for r in range(RD):
        xs_ref[pl.ds(TS * r, TS), :] = x_all[r // per, r % per].astype(F32)
    current = xs_ref[...]
    for r in range(RD):
        sh_ref[pl.ds(TS * r, 1), :] = shift_all[pl.ds(slot_ref[me_r * RD + r], 1), :]
    wide, _ = iota2(current.shape)
    before = jnp.where((wide & 3) == 0, sh_ref[...], pltpu.roll(current, 1, 0))
    towards = before - current
    mixed_in = [(current + towards * blend_ref[b : b + 1, :]).astype(BF16) for b in range(5)]
    d_part = dot_t(mixed_in[1], fn_ref[...])
    l_part = dot_t(mixed_in[4], cn_ref[...])
    loads[8].wait()
    r_part = dot(mixed_in[0], w_ref[0])
    k_part = dot(mixed_in[2], w_ref[1])
    fill = jnp.zeros((TOK, 128 - DL), F32)
    part = jnp.concatenate([r_part, k_part, d_part, fill, l_part, fill], axis=1)
    part_send[...] = part.astype(BF16).reshape(part_send.shape)
    ptc = [send(part_send.at[peer("row", d)], part_recv.at[d - 1], spt, rpt, "row", d) for d in range(1, Z)]
    row, col = iota2((512, 512))
    to_rows = as_ones(
        (((row >> 4) & 3) == (col >> 7)) & ((row >> 6) == ((col >> 4) & 7)) & ((row & 15) == (col & 15))
    )
    v_part = dot(dot(mixed_in[3], w_ref[2]).astype(BF16), to_rows)
    for q in range(Z):
        v_send[q] = v_part[:, 128 * q : 128 * (q + 1)].astype(BF16)
    vc = [send(v_send.at[peer("row", d)], v_recv.at[d - 1], sv, rv, "row", d) for d in range(1, Z)]

    base = pl.multiple_of(me_r * RD, RD)
    for r in range(RD):
        last_all[pl.ds(base + r, 1), :] = xs_ref[pl.ds(TS * r + jnp.clip(valid_ref[me_r * RD + r] - 1, 0, TS - 1), 1), :]
    lac = [
        send(last_all.at[pl.ds(base, RD)], last_all.at[pl.ds(base, RD)], sla, rla, "req", d)
        for d in range(1, R)
    ]

    row, col = iota2((512, 512))
    same_head = as_ones((row >> 6) == (col >> 6))
    row, col = iota2((512, 128))
    head_to_feature = as_ones((row >> 6) == (col >> 4))
    row, col = iota2((128, 128))
    half_sum = as_ones((row >> 6) == (col >> 6))
    parity_sum = as_ones((row >> 6) == (col & 1))
    block16 = as_ones((row >> 4) == (col >> 4))
    row, col = iota2((128, 1024))
    spread = as_ones((row & 15) == (col >> 6))
    def find(q, found):
        page = slot_ref[q] - here_r
        return tuple(jnp.where(page == p, q, f) for p, f in enumerate(found))

    inv = lax.fori_loop(0, slot_ref.shape[0], find, (jnp.int32(0),) * RD)

    total = part_send[me_z].astype(F32)
    for d in range(1, Z):
        ptc[d - 1].wait_recv()
        total = total + part_recv[d - 1].astype(F32)
    sum_send[...] = total.astype(BF16)
    smc = [send(sum_send, sum_all.at[me_z], ssm, rsm, "row", d) for d in range(1, Z)]
    sum_all[me_z] = sum_send[...]

    for c in loads[9:17]:
        c.wait()
    rc_row = jnp.concatenate([rc8_ref[h : h + 1, :] for h in range(8)], axis=1)
    gg_row = jnp.concatenate([gg8_ref[h : h + 1, :] for h in range(8)], axis=1)

    for c in pgc:
        c.wait_recv()
    for r in range(RD):
        page = slot_ref[me_r * RD + r]
        here = page - me_r * RD
        mine = jnp.logical_and(here >= 0, here < RD)
        own = pages_ref[jnp.clip(here, 0, RD - 1)]
        got = pack_in[page].astype(F32)
        for j in range(8):
            away = got[8 * (j >> 2) : 8 * (j >> 2) + 8, 128 * (j & 3) : 128 * (j & 3) + 128]
            s_ref[j, r] = jnp.where(mine, own[:, 128 * j : 128 * j + 128], away)

    values = v_send[me_z].astype(F32)
    for d in range(1, Z):
        vc[d - 1].wait_recv()
        values = values + v_recv[d - 1].astype(F32)

    for c in smc:
        c.wait_recv()
    sums = sum_all[...].reshape(TOK, sum_all.shape[2]).astype(F32)
    query, key_vec = sums[:, :512], sums[:, 512:1024]
    decay_low = jnp.tanh(sums[:, 1024 : 1024 + DL]).astype(BF16)
    learn_low = sums[:, 1152 : 1152 + DL].astype(BF16)
    z = fo_ref[...] + dot(decay_low, fw_ref[...])
    decay = jnp.exp(-0.6065306597126334 / (1.0 + jnp.exp(-z)))
    y = co_ref[...] + dot(learn_low, cw_ref[...])
    learn = 1.0 / (1.0 + jnp.exp(-y))
    scaled = key_vec * eg_ref[...]
    squares = dot((scaled * scaled).astype(BF16), same_head)
    key_dir = scaled * lax.rsqrt(squares + 1e-6)
    key_adj = key_vec * (1.0 + (learn - 1.0) * ac_ref[...])
    bonus = jnp.where(
        live, dot((query * key_adj * rc_row).astype(BF16), head_to_feature) * values, 0.0
    )
    lane = lax.broadcasted_iota(jnp.int32, (TOK, 128), 1)
    low_half = lane < 64

    def heads_out(ref, a):
        for p in range(4):
            pair = a[:, 128 * p : 128 * p + 128]
            other = pltpu.roll(pair, 64, 1)
            ref[pl.ds(2 * p, TOK, stride=8), :] = jnp.where(low_half, pair, other)
            ref[pl.ds(2 * p + 1, TOK, stride=8), :] = jnp.where(low_half, other, pair)

    heads_out(r_d, jnp.where(live1, query, 0.0))
    heads_out(kd_d, key_dir)
    heads_out(kl_d, jnp.where(live1, -key_dir * learn, 0.0))
    heads_out(ka_d, jnp.where(live1, key_adj, 0.0))
    heads_out(dec_d, jnp.where(live1, decay, 1.0))

    srow, scol = iota2((8, 128))
    own_head = (scol >> 4) == srow
    values3 = values.reshape(RD, TS, 128)
    for t in range(TS):
        kd, kl, ka, dec, rq = (
            ref[...].reshape(RD, TS, 8, 128)[:, t] for ref in (kd_d, kl_d, ka_d, dec_d, r_d)
        )
        vt = jnp.where(own_head[None], jnp.broadcast_to(values3[:, t][:, None, :], (RD, 8, 128)), 0.0)
        v_wide = dot(vt.reshape(RD * 8, 128).astype(BF16), spread)
        now = [s_ref[j] for j in range(8)]
        hit = dot(
            jnp.concatenate([(s * kd).reshape(RD * 8, 128).astype(BF16) for s in now], axis=0), half_sum
        )
        after = []
        for j in range(8):
            removed = hit[128 * j : 128 * j + 128].reshape(RD, 8, 128)
            vj = v_wide[:, 128 * j : 128 * j + 128].reshape(RD, 8, 128)
            s = now[j] * dec + removed * kl + vj * ka
            s_ref[j] = s
            after.append((s * rq).reshape(RD * 8, 128).astype(BF16))
        seen = dot(jnp.concatenate(after, axis=0), parity_sum)
        acc = jnp.zeros((RD, 8, 128), F32)
        for j in range(8):
            pick = own_head & (((scol & 15) >> 1) == j)
            acc = acc + jnp.where(pick[None], seen[128 * j : 128 * j + 128].reshape(RD, 8, 128), 0.0)
        read_ref[pl.ds(t, RD, stride=TS), :] = jnp.sum(acc, axis=1)

    reading = read_ref[...]
    vrows = 16
    mean_own = dot_split(reading, block16) * (1.0 / vrows)
    off = reading - mean_own
    sq_own = dot_split(off * off, block16)
    is_mean = (lane & 8) == 0
    slot_here = (lane & 7) == (trow & 7)
    packed = jnp.where(slot_here, jnp.where(is_mean, mean_own, sq_own), 0.0)
    stat_send[...] = jnp.sum(packed.reshape(TOK // 8, 8, 128), axis=1)
    stc = [send(stat_send, stat_recv.at[d - 1], sst, rst, "row", d) for d in range(1, Z)]

    for r in range(RD):
        lo = jnp.concatenate([s_ref[j, r] for j in range(4)], axis=1)
        hi = jnp.concatenate([s_ref[j, r] for j in range(4, 8)], axis=1)
        back_out[r] = jnp.concatenate([lo, hi], axis=0).astype(BF16)
    bkc = [send(back_out, back_in.at[pl.ds(me_r * RD, RD)], sbk, rbk, "req", d) for d in range(1, R)]

    packs = [stat_send[...]]
    for d in range(1, Z):
        stc[d - 1].wait_recv()
        packs.append(stat_recv[d - 1])
    both = sum(packs)
    center = both * (1.0 / Z)
    between = sum([(p - center) * (p - center) for p in packs]) * vrows
    spread_all = (both + pltpu.roll(between, 8, 1)) * (1.0 / (vrows * Z))
    _, plane = iota2(both.shape)
    both = jnp.where((plane & 8) == 0, center, lax.rsqrt(spread_all + 64e-5))
    both = jnp.broadcast_to(both[:, None, :], (TOK // 8, 8, 128)).reshape(TOK, 128)
    mean = dot_split(jnp.where(slot_here & is_mean, both, 0.0), block16)
    scale = dot_split(jnp.where(slot_here & jnp.logical_not(is_mean), both, 0.0), block16)
    normed = ((reading - mean) * scale * gg_row + bonus).astype(BF16)

    loads[17].wait()
    for q in range(Z):
        block = dot(normed, fp_ref[:, 512 * q : 512 * (q + 1)]).astype(BF16)
        for b in range(H):
            out_send[b, q] = block[BT * b : BT * (b + 1)]
    oc = [send(out_send.at[peer("head", d)], out_recv.at[d - 1], so, ro, "head", d) for d in range(1, H)]

    acc = out_send[me_h].astype(F32)
    for d in range(1, H):
        oc[d - 1].wait_recv()
        acc = acc + out_recv[d - 1].astype(F32)
    fin_send[...] = acc.astype(BF16)
    fc = [send(fin_send.at[peer("row", d)], fin_recv.at[d - 1], sf, rf, "row", d) for d in range(1, Z)]
    for c in bkc + lac:
        c.wait_recv()
    for p in range(RD):
        q = inv[p]
        here = q - me_r * RD
        mine = jnp.logical_and(here >= 0, here < RD)
        at = jnp.clip(here, 0, RD - 1)
        got = back_in[q].astype(F32)
        for j in range(8):
            away = got[8 * (j >> 2) : 8 * (j >> 2) + 8, 128 * (j & 3) : 128 * (j & 3) + 128]
            state_buf[p, :, 128 * j : 128 * j + 128] = jnp.where(mine, s_ref[j, at], away)
        shift_out[pl.ds(p, 1), :] = last_all[pl.ds(q, 1), :]

    stored = pltpu.make_async_copy(state_buf, state_out, local_sem.at[18])
    stored.start()

    res = fin_send[me_z].astype(F32)
    for d in range(1, Z):
        fc[d - 1].wait_recv()
        res = res + fin_recv[d - 1].astype(F32)
    for i in range(mixed_ref.shape[0]):
        mixed_ref[i] = res[TS * i : TS * (i + 1)].astype(BF16)
    stored.wait()
    for c in pending:
        c.wait_send()


def hand_on(a, b, c, a_out, b_out, c_out, a_mid, b_mid, c_mid, sem_in, sem_out):
    order = [(b, b_mid, b_out), (a, a_mid, a_out), (c, c_mid, c_out)]
    into = [pltpu.make_async_copy(s, m, sem_in.at[i]) for i, (s, m, _) in enumerate(order)]
    out = [pltpu.make_async_copy(m, o, sem_out.at[i]) for i, (_, m, o) in enumerate(order)]
    for copy in into:
        copy.start()
    for first, then in zip(into, out):
        first.wait()
        then.start()
    for copy in out:
        copy.wait()


def per_device(x, valid, slots, pages, shift, blend, w, fn, fw, fo, cn, cw, co, eg, ac, rc, gg, fp):
    R, H, Z = lax.axis_size("req"), lax.axis_size("head"), lax.axis_size("row")
    RD, heads, flat = pages.shape
    wide = shift.shape[1]
    TOK = RD * TS
    BT, ZT = TOK // H, TOK // Z
    feats = gg.shape[0] * gg.shape[1]
    cols = w.shape[2]
    sums = 2 * cols + 256
    vm = pl.BlockSpec(memory_space=pltpu.VMEM)
    hbm = pl.BlockSpec(memory_space=pltpu.HBM)
    V = pltpu.VMEM
    sems = []
    for n in (H, R, R, Z, Z, Z, Z, H, Z, R, R):
        sems += [pltpu.SemaphoreType.DMA((max(n - 1, 1),))] * 2
    fn, cn = fn.T, cn.T
    vec = (1, cols)
    scratch = [
        pltpu.SMEM(valid.shape, jnp.int32), pltpu.SMEM(slots.shape, jnp.int32),
        V(blend.shape, F32), V(fn.shape, BF16), V(fw.shape, BF16), V(vec, F32),
        V(cn.shape, BF16), V(cw.shape, BF16), V(vec, F32), V(vec, F32), V(vec, F32),
        V(rc.shape, F32), V(gg.shape, F32),
        V(w.shape, BF16), V(pages.shape, F32), V((feats, fp.shape[2]), BF16),
        V(pages.shape, F32),
        V((H,) + x.shape, BF16), V((R * RD, wide), F32),
        V((RD, 2 * heads, flat // 2), BF16), V((R * RD, 2 * heads, flat // 2), BF16),
        V((TOK, wide), F32), V((TOK, wide), F32), V((TOK, 128), jnp.int32),
        V((Z, ZT, sums), BF16), V((Z - 1, ZT, sums), BF16),
        V((Z, TOK, feats), BF16), V((Z - 1, TOK, feats), BF16),
        V((ZT, sums), BF16), V((Z, ZT, sums), BF16),
        V((TOK * 8, 128), F32), V((TOK * 8, 128), F32), V((TOK * 8, 128), F32),
        V((TOK * 8, 128), F32), V((TOK * 8, 128), F32),
        V((8, RD, 8, 128), F32), V((TOK, 128), F32),
        V((RD, 2 * heads, flat // 2), BF16), V((R * RD, 2 * heads, flat // 2), BF16),
        V((R * RD, wide), F32),
        V((TOK // 8, 128), F32), V((Z - 1, TOK // 8, 128), F32),
        V((H, Z, BT, wide), BF16), V((H - 1, Z, BT, wide), BF16),
        V((Z, BT, wide), BF16), V((Z - 1, BT, wide), BF16),
        pltpu.SemaphoreType.DMA((19,)),
    ] + sems
    results = pl.pallas_call(
        functools.partial(kernel, (R, H, Z)),
        out_shape=(
            jax.ShapeDtypeStruct(x.shape, BF16),
            jax.ShapeDtypeStruct(pages.shape, F32),
            jax.ShapeDtypeStruct(shift.shape, F32),
        ),
        in_specs=[hbm] * 18,
        out_specs=(vm, hbm, vm),
        scratch_shapes=scratch,
        compiler_params=pltpu.CompilerParams(
            collective_id=0, has_side_effects=True, vmem_limit_bytes=63 * 1024 * 1024
        ),
    )(
        valid, slots, x, pages, shift, blend, w, fn, fw,
        fo.reshape(1, -1), cn, cw, co.reshape(1, -1), eg.reshape(1, -1), ac.reshape(1, -1),
        rc, gg, fp.reshape(feats, -1),
    )
    return pl.pallas_call(
        hand_on,
        out_shape=tuple(jax.ShapeDtypeStruct(a.shape, a.dtype) for a in results),
        in_specs=[hbm] * 3,
        out_specs=(hbm,) * 3,
        scratch_shapes=[V(a.shape, a.dtype) for a in results] + [pltpu.SemaphoreType.DMA((3,))] * 2,
        compiler_params=pltpu.CompilerParams(vmem_limit_bytes=63 * 1024 * 1024),
    )(*results)


def solution(mesh):
    placed = (
        P(("req", "head"), None, "row"),
        P(),
        P(),
        P("req", "head", "row"),
        P("req", "row"),
        P(None, "row"),
        P(None, "row", "head"),
        P("row", None),
        P(None, "head"),
        P("head"),
        P("row", None),
        P(None, "head"),
        P("head"),
        P("head"),
        P("head"),
        P("head", None),
        P("head", "row"),
        P("head", "row", None),
    )
    return jax.shard_map(
        per_device,
        mesh=mesh,
        in_specs=placed,
        out_specs=(P(("req", "head"), None, "row"), P("req", "head", "row"), P("req", "row")),
        check_vma=False,
    )
```
